512 devices in a mesh: dp: 128 (over x, z, core), tensor: 4 (over y).
Axes of the slice: x: 4, y: 4, z: 16, core: 2. Of those that a mesh axis runs over, the one named last changes fastest.
Arguments:
- tokens: bfloat16 [32768, 2048], P('dp', 'tensor'), may hold values from -6 to 6
- expert_ids: int32 [32768, 2], P('dp'), may hold values from 0 to 127, as said below
- route_weights: float32 [32768, 2], P('dp'), may hold values from 0.2 to 1
- gate_weight: bfloat16 [128, 2048, 1024], P('dp', None, 'tensor'), may hold values from -0.125 to 0.125
- up_weight: bfloat16 [128, 2048, 1024], P('dp', None, 'tensor'), may hold values from -0.125 to 0.125
- down_weight: bfloat16 [128, 1024, 2048], P('dp', 'tensor'), may hold values from -0.1875 to 0.1875
Outputs:
- moe_out: bfloat16 [32768, 2048], P('dp', 'tensor')
The draws below stay inside these ranges and needn't reach their ends.
Inputs may be any that keep to these rules, and one draw needn't show every extreme that they name: `expert_ids`: the two experts of a row differ. Among the rows of one index of dp, no expert is named more than 8 times.
All inputs are finite; a program needn't handle non-finite values.
Results may differ from the reference program's by a relative error of at most 0.011.
Values may be sent and summed in bfloat16 or wider, within the bound.
A program may use at most 64 MiB of HBM per device.

```python
import jax
import jax.numpy as jnp
from jax import lax

D = 2048
FF = 1024
TOP = 2
TOK_DEV = 256
EXPERTS = 128
TOKENS = 32768
CAP = 8
N_DP = 128
N_TENSOR = 4


def draw_expert_ids(key, part):
    blocks = TOKENS // TOK_DEV
    key_weight, key_hot, key_noise, key_count, key_shuffle = jax.random.split(key, 5)
    popularity = jax.random.randint(key_weight, (EXPERTS,), 1, 9)
    hot_expert = jax.random.randint(key_hot, (), 0, EXPERTS)
    numbers = jnp.arange(EXPERTS, dtype=jnp.int32)
    noise_draw = jax.random.randint(key_noise, (blocks, EXPERTS), 0, 1 << 16)
    scores = noise_draw * popularity[None, :] * EXPERTS + numbers[None, :]
    scores = jnp.where(numbers[None, :] == hot_expert, 1 << 30, scores)
    unused_values, ranked = lax.top_k(scores, EXPERTS)
    least_count = (2 * TOK_DEV - CAP + EXPERTS - 2) // (EXPERTS - 1)
    run_counts = jax.random.randint(key_count, (blocks, EXPERTS), least_count, CAP + 1)
    run_counts = run_counts.at[:, 0].set(CAP)
    run_ends = jnp.cumsum(run_counts, axis=1)
    slot_numbers = jnp.arange(2 * TOK_DEV, dtype=jnp.int32)
    run_index = jnp.sum((slot_numbers[None, :, None] >= run_ends[:, None, :]).astype(jnp.int32), axis=2)
    named = jnp.take_along_axis(ranked, run_index, axis=1)
    paired = jnp.stack([named[:, :TOK_DEV], named[:, TOK_DEV:]], axis=2)
    shuffle_keys = jax.random.split(key_shuffle, blocks)
    shuffled = jax.vmap(lambda one_key: jax.random.permutation(one_key, TOK_DEV))(shuffle_keys)
    paired = jnp.take_along_axis(paired, shuffled[:, :, None], axis=1)
    return paired.reshape(TOKENS, 2).astype(jnp.int32)


def levels(own_key, extent, shards, low, largest):
    def one(dim, parts):
        heights = jax.random.uniform(jax.random.fold_in(jax.random.fold_in(own_key, 6), dim), (parts,), jnp.float32, low / len(shards), largest / len(shards))
        return jnp.repeat(jnp.exp(heights), extent[dim] // parts).reshape((-1,) + (1,) * (len(extent) - dim - 1))

    factor_of = one(*shards[0])
    for cut in shards[1:]:
        factor_of = factor_of * one(*cut)
    return factor_of


def normal_values(rng, extent, deviation, most, cuts=(), kind=jnp.bfloat16):
    entries = deviation * jax.random.normal(rng, extent, jnp.float32)
    if cuts:
        entries = entries * levels(rng, extent, cuts, -0.22, 0.18)
    return jnp.clip(entries, -most, most).astype(kind)


def setup_inputs(seed: int = 0) -> dict:
    seeds = jax.random.split(jax.random.key(seed), 7)
    return {
        "tokens": normal_values(seeds[0], (TOKENS, D), 1.0, 6.0, ((0, 128), (1, 4))),
        "expert_ids": draw_expert_ids(jax.random.fold_in(seeds[6], 71), 0),
        "route_weights": jnp.clip(0.2 + 0.8 * jax.random.uniform(seeds[2], (TOKENS, TOP), jnp.float32) ** levels(seeds[2], (TOKENS, TOP), ((0, 128),), -0.2, 0.2), 0.2, 1.0),
        "gate_weight": normal_values(seeds[3], (EXPERTS, D, FF), D ** -0.5, 0.125, ((0, 128), (2, 4))),
        "up_weight": normal_values(seeds[4], (EXPERTS, D, FF), D ** -0.5, 0.125, ((0, 128), (2, 4))),
        "down_weight": normal_values(seeds[5], (EXPERTS, FF, D), FF ** -0.5, 0.1875, ((0, 128), (1, 4))),
    }


def reference(tokens, expert_ids, route_weights, gate_weight, up_weight, down_weight):
    chosen = expert_ids.reshape(-1).astype(jnp.int32)
    assignments = chosen.shape[0]
    token_order = jnp.argsort(chosen, stable=True).astype(jnp.int32)
    counts = jax.ops.segment_sum(jnp.ones((assignments,), jnp.int32), chosen, num_segments=EXPERTS).astype(jnp.int32)
    starts = (jnp.cumsum(counts) - counts).astype(jnp.int32)
    most_rows = N_DP * CAP
    padded = jnp.concatenate([token_order, jnp.zeros((most_rows,), jnp.int32)])
    quarter = FF // N_TENSOR

    def expert_out(expert):
        picked = lax.dynamic_slice(padded, (starts[expert].astype(jnp.int32),), (most_rows,))
        token_rows = tokens[picked // 2]
        gate_value = jnp.dot(token_rows, gate_weight[expert], preferred_element_type=jnp.float32)
        up_value = jnp.dot(token_rows, up_weight[expert], preferred_element_type=jnp.float32)
        hidden = (jax.nn.silu(gate_value) * up_value).astype(jnp.bfloat16)
        summed = jnp.zeros((most_rows, D), jnp.float32)
        for share_index in range(N_TENSOR):
            lower = share_index * quarter
            partial_sum = jnp.dot(hidden[:, lower:lower + quarter], down_weight[expert, lower:lower + quarter], preferred_element_type=jnp.float32)
            rounded = lax.optimization_barrier(partial_sum.astype(jnp.bfloat16))
            summed = summed + rounded.astype(jnp.float32)
        return summed.astype(jnp.bfloat16)

    outputs = lax.map(expert_out, jnp.arange(EXPERTS, dtype=jnp.int32))
    position = jnp.zeros((assignments,), jnp.int32).at[token_order].set(jnp.arange(assignments, dtype=jnp.int32))
    rank_in = (position - starts[chosen]).astype(jnp.int32)
    gathered = outputs[chosen, rank_in]
    weighted = gathered.astype(jnp.float32).reshape(-1, TOP, D) * route_weights[:, :, None]
    return jnp.sum(weighted, axis=1).astype(jnp.bfloat16)
```

```python
import jax
import jax.numpy as jnp
from jax import lax
from jax.experimental import pallas as pl
from jax.experimental.pallas import tpu as pltpu
from jax.sharding import PartitionSpec as P

MESH = pl.DeviceIdType.MESH
BF = jnp.bfloat16
F32 = jnp.float32
TOK = 256
WID = 512
CUT = 2
NEAR = 4
PAIRS = 8
FAR_ROWS = 224


def dot(a, b):
    return jnp.dot(a, b, preferred_element_type=F32)


def dot_t(a, b):
    return lax.dot_general(a, b, (((0,), (0,)), ((), ())), preferred_element_type=F32)


def kernel(
    tok, ids, rw, gate_hbm, up_hbm, down_hbm, out,
    TR, MO, MT, PK, FS, FR, F, Wg, Wu, Wd, ST, Hd, O, R, DI, FB, CB, CO, RA, RO,
    wl, zs, zr, ms, mr, fs, fr, ps, pr, ys, yr, hs, hr, ds, dr, qs, qr, bs, br, rs, rr,
):
    dp = lax.axis_index("dp")
    y = lax.axis_index("tensor")
    x, z, c = dp // 32, (dp // 2) % 16, dp % 2
    m = x * 2 + c

    def at(x1, z1, c1):
        return ((x1 * 16 + z1) * 2 + c1, y)

    def along_z(d, h):
        return at(x, (z + (h if d == 0 else 16 - h)) % 16, c)

    def in_plane(j):
        k = (m + j) % 8
        return k, at(k // 2, z, k % 2)

    y_next = [(dp, (y + 1) % 4), (dp, (y + 3) % 4)]
    sent = []

    def send(src, dst, s, r, dev):
        copy = pltpu.make_async_remote_copy(
            src_ref=src, dst_ref=dst, send_sem=s, recv_sem=r, device_id=dev, device_id_type=MESH
        )
        copy.start()
        sent.append(copy.wait_send)

    def got(dst, r):
        pltpu.make_async_copy(dst, dst, r).wait()

    def drain():
        while sent:
            sent.pop()()

    loads = [
        pltpu.make_async_copy(gate_hbm.at[0], Wg, wl.at[0]),
        pltpu.make_async_copy(up_hbm.at[0], Wu, wl.at[1]),
        pltpu.make_async_copy(down_hbm.at[0, :, pl.ds(pl.multiple_of(y * WID, WID), WID)], Wd.at[y], wl.at[2]),
    ]
    for load in loads:
        load.start()

    barrier = pltpu.get_barrier_semaphore()
    peers = [along_z(d, h) for d in (0, 1) for h in range(1, NEAR + 1)]
    peers += [in_plane(j)[1] for j in range(1, 8)] + y_next
    for dev in peers:
        pl.semaphore_signal(barrier, inc=1, device_id=dev, device_id_type=MESH)
    pl.semaphore_wait(barrier, len(peers))

    part = TOK // CUT

    def piece(ref, k):
        return ref.at[pl.ds(k * part, part)]

    def z_send(d, h, k):
        src = tok if h == 0 else TR.at[d, h - 1]
        send(piece(src, k), piece(TR.at[d, h], k), zs.at[d, h, k], zr.at[d, h, k], along_z(d, 1))

    for k in range(CUT):
        for d in (0, 1):
            z_send(d, 0, k)

    def columns(j):
        return pl.ds(pl.multiple_of(((y + j) % 4) * WID, WID), WID)

    for d in (0, 1):
        send(down_hbm.at[0, pl.ds(d * 128, 128), columns(2)], ST.at[d], ds.at[d], dr.at[d], y_next[d])
    for d in (0, 1):
        send(down_hbm.at[0, :, columns((1, 3)[d])], Wd.at[y], ds.at[2 + d], dr.at[2 + d], y_next[d])

    row = lax.broadcasted_iota(jnp.int32, (128, TOK), 0)
    hot = [(row == ids[k : k + 1, :]).astype(F32) for k in (0, 1)]
    before = (
        lax.broadcasted_iota(jnp.int32, (TOK, TOK), 0) < lax.broadcasted_iota(jnp.int32, (TOK, TOK), 1)
    ).astype(F32).astype(BF)
    count = [dot(hot[k].astype(BF), before) for k in (0, 1)]
    count[1] = count[1] + jnp.sum(hot[0], axis=1, keepdims=True)
    MO[...] = jnp.zeros((8, TOK), F32)
    for k in (0, 1):
        e = ids[k : k + 1, :]
        rank = jnp.sum(hot[k] * count[k], axis=0, keepdims=True)
        place = ((e >> 1) & 15) * 64 + ((e >> 5) * 2 + (e & 1)) * 8
        MO[k : k + 1, :] = place.astype(F32) + rank
        MO[2 + k : 3 + k, :] = rw[k : k + 1, :]
    for h in range(NEAR):
        for d in (0, 1):
            send(MO, MT.at[d, h], ms.at[d, h], mr.at[d, h], along_z(d, h + 1))

    def pair_target():
        r = lax.broadcasted_iota(jnp.int32, (128, TOK), 0)
        return (z * 64 + (r >> 4) * 8 + (r & 7)).astype(F32), (r >> 3) & 1

    def far_target(d):
        r = lax.broadcasted_iota(jnp.int32, (FAR_ROWS, TOK), 0)
        step = (r >> 6) + 1
        station = (z + (step if d == 0 else 16 - step)) & 15
        within = r & 63
        if d == 1:
            within = jnp.where(r >= 192, within + 32, within)
        return (station * 64 + within).astype(F32)

    def chosen(meta, target):
        return (meta[0:1, :] == target) | (meta[1:2, :] == target)

    def weights(meta, target, keep=None):
        w = jnp.where(meta[0:1, :] == target, meta[2:3, :], 0.0) + jnp.where(
            meta[1:2, :] == target, meta[3:4, :], 0.0
        )
        if keep is not None:
            w = jnp.where(keep, w, 0.0)
        high = w.astype(BF)
        return high, (w - high.astype(F32)).astype(BF)

    def mix(w, rows):
        return dot_t(w[0], rows) + dot_t(w[1], rows)

    def as_hot(mask):
        return jnp.where(mask, 1.0, 0.0).astype(BF)

    def select(meta, rows, d):
        target, side = pair_target()
        return dot(as_hot(chosen(meta, target) & (side == d)), rows)

    def to_plane(q):
        for j in range(1, 8):
            k, dev = in_plane(j)
            src = PK.at[q, pl.ds(pl.multiple_of(k * 16, 16), 16)]
            dst = F.at[q, y, pl.ds(pl.multiple_of(m * 16, 16), 16)]
            pltpu.make_async_remote_copy(
                src_ref=src, dst_ref=dst, send_sem=ps.at[q], recv_sem=pr.at[q], device_id=dev, device_id_type=MESH
            ).start()
        mine = pl.ds(pl.multiple_of(m * 16, 16), 16)
        F[q, y, mine, :] = PK[q, mine, :]
        sent.append(lambda: got(PK.at[q, pl.ds(0, 112)], ps.at[q]))

    def S0(q):
        if 1 <= q <= NEAR:
            pick = select(MT[0, q - 1], TR[0, q - 1], 0) + select(MT[1, q - 1], TR[1, q - 1], 1)
        else:
            r = lax.broadcasted_iota(jnp.int32, (128, 128), 0)
            k = lax.broadcasted_iota(jnp.int32, (128, 128), 1)
            slot, side = (r >> 4) * 8 + (r & 7), (r >> 3) & 1
            j = (q - 5) % 8
            if q:
                for d in (0, 1):
                    got(FR.at[j, pl.ds(d * 64, 64)], fr.at[d, j])
                pick = dot(as_hot(k == side * 64 + slot), FR[j])
            else:
                for d in (0, 1):
                    got(FR.at[j, pl.ds(d * 32, 32)], fr.at[d, j])
                pick = dot(as_hot((k == slot) & (side == 1)[:, :])[:, :64], FR[j, :64]) + PK[0].astype(F32)
        PK[q] = pick.astype(BF)
        to_plane(q)

    def gather_first(q, buf, s, r):
        for d in (0, 1):
            send(buf.at[q, y], buf.at[q, y], s.at[q, d], r.at[q, d], y_next[d])

    def gather_second(q, buf, s, r):
        for d in (0, 1):
            origin = (y + (3, 1)[d]) % 4
            got(buf.at[q, origin], r.at[q, d])
            half = buf.at[q, origin, pl.ds(d * 64, 64)]
            send(half, half, s.at[q, 2 + d], r.at[q, 2 + d], y_next[d])

    def gather_wait(q, buf, r):
        for d in (0, 1):
            got(buf.at[q, (y + 2) % 4, pl.ds(d * 64, 64)], r.at[q, 2 + d])

    def S1(q):
        got(F.at[q, y, pl.ds(0, 112)], pr.at[q])
        gather_first(q, F, ys, yr)

    def S2(q):
        gather_second(q, F, ys, yr)

    def S3(q):
        gather_wait(q, F, yr)
        g = jnp.zeros((128, 256), F32)
        u = jnp.zeros((128, 256), F32)
        for k in range(4):
            rows = F[q, k]
            g = g + dot(rows, Wg[k * WID : (k + 1) * WID, :])
            u = u + dot(rows, Wu[k * WID : (k + 1) * WID, :])
        Hd[q, y] = (g / (1.0 + jnp.exp(-g)) * u).astype(BF)

    def H(q):
        gather_first(q, Hd, hs, hr)

    def S4(q):
        gather_second(q, Hd, hs, hr)

    def S5(q):
        gather_wait(q, Hd, hr)
        o = jnp.zeros((128, WID), F32)
        for k in range(4):
            o = o + dot(Hd[q, k], Wd[k])
        O[q] = o.astype(BF)
        for j in range(1, 8):
            k, dev = in_plane(j)
            src = O.at[q, pl.ds(pl.multiple_of(k * 16, 16), 16)]
            dst = R.at[q, pl.ds(pl.multiple_of(m * 16, 16), 16)]
            pltpu.make_async_remote_copy(
                src_ref=src, dst_ref=dst, send_sem=qs.at[q], recv_sem=qr.at[q], device_id=dev, device_id_type=MESH
            ).start()
        mine = pl.ds(pl.multiple_of(m * 16, 16), 16)
        R[q, mine, :] = O[q, mine, :]
        sent.append(lambda: got(O.at[q, pl.ds(0, 112)], qs.at[q]))

    def S6(q):
        got(R.at[q, pl.ds(0, 112)], qr.at[q])
        if 1 <= q <= NEAR:
            target, side = pair_target()
            for d in (0, 1):
                CB[d, q - 1] = mix(weights(MT[d, q - 1], target, side == d), R[q])
            return
        k = lax.broadcasted_iota(jnp.int32, (128, 128), 0)
        r = lax.broadcasted_iota(jnp.int32, (128, 128), 1)
        slot, side = (r >> 4) * 8 + (r & 7), (r >> 3) & 1
        j = (q - 5) % 8
        DI[j] = dot(as_hot(k == side * 64 + slot), R[q]).astype(BF)
        for d in (0, 1):
            if q:
                rows, to = pl.ds(d * 64, 64), pl.ds(j * 64, 64)
            else:
                rows, to = pl.ds(64 + d * 32, 32), pl.ds(192, 32)
            send(DI.at[j, rows], FB.at[d, to], bs.at[d, j], br.at[d, j], along_z(1 - d, j + 1))

    def arrive(h, k):
        for d in (0, 1):
            got(piece(TR.at[d, h - 1], k), zr.at[d, h - 1, k])
            if h < NEAR:
                z_send(d, h, k)

    def round_of(h, between):
        arrive(h, 0)
        between()
        arrive(h, 1)
        for d in (0, 1):
            got(MT.at[d, h - 1], mr.at[d, h - 1])
        if h == NEAR:
            for d in (0, 1):
                FS[d] = dot(as_hot(chosen(MT[d, h - 1], far_target(d))), TR[d, h - 1]).astype(BF)
            for j in range(3, -1, -1):
                for d in (0, 1):
                    rows = pl.ds(j * 64, 64 if j < 3 else 32)
                    to = pl.ds(d * 64, 64) if j < 3 else pl.ds(d * 32, 32)
                    send(FS.at[d, rows], FR.at[j, to], fs.at[d, j], fr.at[d, j], along_z(d, j + 1))
        S0(h)

    PK[0] = select(MO[...], tok[...], 0).astype(BF)

    def forward_down():
        for d in (0, 1):
            got(ST.at[d], dr.at[d])
            send(ST.at[d], Wd.at[(y + (3, 1)[d]) % 4, pl.ds(d * 128, 128)], ds.at[4 + d], dr.at[4 + d], y_next[d])

    round_of(1, lambda: None)
    forward_down()
    round_of(2, lambda: S1(1))
    for load in loads:
        load.wait()
    round_of(3, lambda: S1(2))
    S2(1)
    round_of(4, lambda: S1(3))
    S2(2), S3(1)
    S0(5), S1(4), S2(3), S3(2)
    S0(6), S1(5), S2(4), S3(3)
    S0(7), S1(6), S2(5), S3(4)
    S0(0), S1(7), S2(6), S3(5), H(5)
    S1(0), S2(7), S3(6), H(6), S4(5)
    for d in (0, 1):
        got(Wd.at[(y + (3, 1)[d]) % 4], dr.at[2 + d])
        got(Wd.at[(y + 2) % 4, pl.ds(d * 128, 128)], dr.at[4 + d])
    S2(0), S3(7), H(7), S4(6), S5(5)
    S3(0), H(0), S4(7), S5(6), S6(5)
    H(4)
    S4(0), S5(7), S6(6)
    S4(4), H(3), H(2), H(1)
    S5(0), S6(7)
    S5(4), S6(0)
    S4(3), S6(4)
    S5(3), S4(2), S4(1)
    drain()

    def back(d, h, k, value):
        RO[d, h - 1, k * part : (k + 1) * part, :] = value.astype(BF)
        send(
            piece(RO.at[d, h - 1], k), piece(RA.at[d, h - 1], k), rs.at[d, h - 1, k], rr.at[d, h - 1, k], along_z(1 - d, 1)
        )

    for d in (0, 1):
        for j in range(4):
            to = pl.ds(j * 64, 64) if j < 3 else pl.ds(192, 32)
            got(FB.at[d, to], br.at[d, j])
        total = CB[d, NEAR - 1] + mix(weights(MT[d, NEAR - 1], far_target(d)), FB[d])
        for k in range(CUT):
            back(d, NEAR, k, total[k * part : (k + 1) * part])
    S6(3), S5(2), S5(1)

    def inwards(h):
        for k in range(CUT):
            for d in (0, 1):
                got(piece(RA.at[d, h], k), rr.at[d, h, k])
                rows = slice(k * part, (k + 1) * part)
                back(d, h, k, RA[d, h, rows, :].astype(F32) + CB[d, h - 1, rows, :])

    inwards(3)
    S6(2)
    inwards(2)
    S6(1)
    inwards(1)
    target, side = pair_target()
    CO[...] = mix(weights(MO[...], target, side == 0), R[0])
    drain()
    for k in range(CUT):
        for d in (0, 1):
            got(piece(RA.at[d, 0], k), rr.at[d, 0, k])
        rows = slice(k * part, (k + 1) * part)
        out[rows, :] = (
            CO[rows, :] + RA[0, 0, rows, :].astype(F32) + RA[1, 0, rows, :].astype(F32)
        ).astype(BF)


def body(tokens, expert_ids, route_weights, gate_weight, up_weight, down_weight):
    vmem = pl.BlockSpec(memory_space=pltpu.VMEM)
    hbm = pl.BlockSpec(memory_space=pl.ANY)
    V, DMA = pltpu.VMEM, pltpu.SemaphoreType.DMA
    scratch = [
        V((2, NEAR, TOK, WID), BF),
        V((8, TOK), F32),
        V((2, NEAR, 8, TOK), F32),
        V((PAIRS, 128, WID), BF),
        V((2, FAR_ROWS, WID), BF),
        V((4, 128, WID), BF),
        V((PAIRS, 4, 128, WID), BF),
        V((2048, 256), BF),
        V((2048, 256), BF),
        V((4, 256, WID), BF),
        V((2, 128, WID), BF),
        V((PAIRS, 4, 128, 256), BF),
        V((PAIRS, 128, WID), BF),
        V((PAIRS, 128, WID), BF),
        V((4, 128, WID), BF),
        V((2, FAR_ROWS, WID), BF),
        V((2, NEAR, TOK, WID), F32),
        V((TOK, WID), F32),
        V((2, NEAR, TOK, WID), BF),
        V((2, NEAR, TOK, WID), BF),
        DMA((3,)),
        DMA((2, NEAR, CUT)), DMA((2, NEAR, CUT)),
        DMA((2, NEAR)), DMA((2, NEAR)),
        DMA((2, 4)), DMA((2, 4)),
        DMA((PAIRS,)), DMA((PAIRS,)),
        DMA((PAIRS, 4)), DMA((PAIRS, 4)),
        DMA((PAIRS, 4)), DMA((PAIRS, 4)),
        DMA((6,)), DMA((6,)),
        DMA((PAIRS,)), DMA((PAIRS,)),
        DMA((2, 4)), DMA((2, 4)),
        DMA((2, NEAR, CUT)), DMA((2, NEAR, CUT)),
    ]
    return pl.pallas_call(
        kernel,
        out_shape=jax.ShapeDtypeStruct((TOK, WID), BF),
        in_specs=[vmem, vmem, vmem, hbm, hbm, hbm],
        out_specs=vmem,
        scratch_shapes=scratch,
        compiler_params=pltpu.CompilerParams(
            collective_id=0, has_side_effects=True, vmem_limit_bytes=48 * 1024 * 1024
        ),
        cost_estimate=pl.CostEstimate(
            flops=2 * 1024 * 3 * 2048 * 256, bytes_accessed=4 * 1024 * 1024, transcendentals=1024 * 256
        ),
    )(tokens, expert_ids.T, route_weights.T, gate_weight, up_weight, down_weight)


def solution(mesh):
    return jax.shard_map(
        body,
        mesh=mesh,
        in_specs=(
            P("dp", "tensor"),
            P("dp", None),
            P("dp", None),
            P("dp", None, "tensor"),
            P("dp", None, "tensor"),
            P("dp", "tensor", None),
        ),
        out_specs=P("dp", "tensor"),
        check_vma=False,
    )
```

```python
import jax
import jax.numpy as jnp
from jax import lax
from jax.experimental import pallas as pl
from jax.experimental.pallas import tpu as pltpu
from jax.sharding import PartitionSpec as P

MESH = pl.DeviceIdType.MESH
BF = jnp.bfloat16
F32 = jnp.float32
TOK = 256
WID = 512
CUT = 2
NEAR = 4
PAIRS = 8
FAR_ROWS = 224


def dot(a, b):
    return jnp.dot(a, b, preferred_element_type=F32)


def dot_t(a, b):
    return lax.dot_general(a, b, (((0,), (0,)), ((), ())), preferred_element_type=F32)


def kernel(
    tok, ids, rw, gate_hbm, up_hbm, down_hbm, out,
    TR, MO, MT, PK, FS, FR, F, Wg, Wu, Wd, ST, Hd, O, R, DI, FB, CB, CO, RA, RO,
    wl, zs, zr, ms, mr, fs, fr, ps, pr, ys, yr, hs, hr, ds, dr, qs, qr, bs, br, rs, rr,
):
    dp = lax.axis_index("dp")
    y = lax.axis_index("tensor")
    x, z, c = dp // 32, (dp // 2) % 16, dp % 2
    m = x * 2 + c

    def at(x1, z1, c1):
        return ((x1 * 16 + z1) * 2 + c1, y)

    def along_z(d, h):
        return at(x, (z + (h if d == 0 else 16 - h)) % 16, c)

    def in_plane(j):
        k = (m + j) % 8
        return k, at(k // 2, z, k % 2)

    y_next = [(dp, (y + 1) % 4), (dp, (y + 3) % 4)]
    sent = []

    def send(src, dst, s, r, dev):
        copy = pltpu.make_async_remote_copy(
            src_ref=src, dst_ref=dst, send_sem=s, recv_sem=r, device_id=dev, device_id_type=MESH
        )
        copy.start()
        sent.append(copy.wait_send)

    def got(dst, r):
        pltpu.make_async_copy(dst, dst, r).wait()

    def drain():
        while sent:
            sent.pop()()

    loads = [
        pltpu.make_async_copy(gate_hbm.at[0], Wg, wl.at[0]),
        pltpu.make_async_copy(up_hbm.at[0], Wu, wl.at[1]),
        pltpu.make_async_copy(down_hbm.at[0, :, pl.ds(pl.multiple_of(y * WID, WID), WID)], Wd.at[y], wl.at[2]),
    ]
    for load in loads:
        load.start()

    barrier = pltpu.get_barrier_semaphore()
    peers = [along_z(d, h) for d in (0, 1) for h in range(1, NEAR + 1)]
    peers += [in_plane(j)[1] for j in range(1, 8)] + y_next
    for dev in peers:
        pl.semaphore_signal(barrier, inc=1, device_id=dev, device_id_type=MESH)
    pl.semaphore_wait(barrier, len(peers))

    part = TOK // CUT

    def piece(ref, k):
        return ref.at[pl.ds(k * part, part)]

    def z_send(d, h, k):
        src = tok if h == 0 else TR.at[d, h - 1]
        send(piece(src, k), piece(TR.at[d, h], k), zs.at[d, h, k], zr.at[d, h, k], along_z(d, 1))

    for k in range(CUT):
        for d in (0, 1):
            z_send(d, 0, k)

    def columns(j):
        return pl.ds(pl.multiple_of(((y + j) % 4) * WID, WID), WID)

    for d in (0, 1):
        send(down_hbm.at[0, pl.ds(d * 128, 128), columns(2)], ST.at[d], ds.at[d], dr.at[d], y_next[d])
    for d in (0, 1):
        send(down_hbm.at[0, :, columns((1, 3)[d])], Wd.at[y], ds.at[2 + d], dr.at[2 + d], y_next[d])

    row = lax.broadcasted_iota(jnp.int32, (128, TOK), 0)
    hot = [(row == ids[k : k + 1, :]).astype(F32) for k in (0, 1)]
    before = (
        lax.broadcasted_iota(jnp.int32, (TOK, TOK), 0) < lax.broadcasted_iota(jnp.int32, (TOK, TOK), 1)
    ).astype(F32).astype(BF)
    count = [dot(hot[k].astype(BF), before) for k in (0, 1)]
    count[1] = count[1] + jnp.sum(hot[0], axis=1, keepdims=True)
    MO[...] = jnp.zeros((8, TOK), F32)
    for k in (0, 1):
        e = ids[k : k + 1, :]
        rank = jnp.sum(hot[k] * count[k], axis=0, keepdims=True)
        place = ((e >> 1) & 15) * 64 + ((e >> 5) * 2 + (e & 1)) * 8
        MO[k : k + 1, :] = place.astype(F32) + rank
        MO[2 + k : 3 + k, :] = rw[k : k + 1, :]
    for h in range(NEAR):
        for d in (0, 1):
            send(MO, MT.at[d, h], ms.at[d, h], mr.at[d, h], along_z(d, h + 1))

    def pair_target():
        r = lax.broadcasted_iota(jnp.int32, (128, TOK), 0)
        return (z * 64 + (r >> 4) * 8 + (r & 7)).astype(F32), (r >> 3) & 1

    def far_target(d):
        r = lax.broadcasted_iota(jnp.int32, (FAR_ROWS, TOK), 0)
        step = (r >> 6) + 1
        station = (z + (step if d == 0 else 16 - step)) & 15
        within = r & 63
        if d == 1:
            within = jnp.where(r >= 192, within + 32, within)
        return (station * 64 + within).astype(F32)

    def chosen(meta, target):
        return (meta[0:1, :] == target) | (meta[1:2, :] == target)

    def weights(meta, target, keep=None):
        w = jnp.where(meta[0:1, :] == target, meta[2:3, :], 0.0) + jnp.where(
            meta[1:2, :] == target, meta[3:4, :], 0.0
        )
        if keep is not None:
            w = jnp.where(keep, w, 0.0)
        high = w.astype(BF)
        return high, (w - high.astype(F32)).astype(BF)

    def mix(w, rows):
        return dot_t(w[0], rows) + dot_t(w[1], rows)

    def as_hot(mask):
        return jnp.where(mask, 1.0, 0.0).astype(BF)

    def select(meta, rows, d):
        target, side = pair_target()
        return dot(as_hot(chosen(meta, target) & (side == d)), rows)

    def to_plane(q):
        for j in range(1, 8):
            k, dev = in_plane(j)
            src = PK.at[q, pl.ds(pl.multiple_of(k * 16, 16), 16)]
            dst = F.at[q, y, pl.ds(pl.multiple_of(m * 16, 16), 16)]
            pltpu.make_async_remote_copy(
                src_ref=src, dst_ref=dst, send_sem=ps.at[q], recv_sem=pr.at[q], device_id=dev, device_id_type=MESH
            ).start()
        mine = pl.ds(pl.multiple_of(m * 16, 16), 16)
        F[q, y, mine, :] = PK[q, mine, :]
        sent.append(lambda: got(PK.at[q, pl.ds(0, 112)], ps.at[q]))

    def S0(q):
        if 1 <= q <= NEAR:
            pick = select(MT[0, q - 1], TR[0, q - 1], 0) + select(MT[1, q - 1], TR[1, q - 1], 1)
        else:
            r = lax.broadcasted_iota(jnp.int32, (128, 128), 0)
            k = lax.broadcasted_iota(jnp.int32, (128, 128), 1)
            slot, side = (r >> 4) * 8 + (r & 7), (r >> 3) & 1
            j = (q - 5) % 8
            if q:
                for d in (0, 1):
                    got(FR.at[j, pl.ds(d * 64, 64)], fr.at[d, j])
                pick = dot(as_hot(k == side * 64 + slot), FR[j])
            else:
                for d in (0, 1):
                    got(FR.at[j, pl.ds(d * 32, 32)], fr.at[d, j])
                pick = dot(as_hot((k == slot) & (side == 1)[:, :])[:, :64], FR[j, :64]) + PK[0].astype(F32)
        PK[q] = pick.astype(BF)
        to_plane(q)

    def gather_first(q, buf, s, r):
        for d in (0, 1):
            send(buf.at[q, y], buf.at[q, y], s.at[q, d], r.at[q, d], y_next[d])

    def gather_second(q, buf, s, r):
        for d in (0, 1):
            origin = (y + (3, 1)[d]) % 4
            got(buf.at[q, origin], r.at[q, d])
            half = buf.at[q, origin, pl.ds(d * 64, 64)]
            send(half, half, s.at[q, 2 + d], r.at[q, 2 + d], y_next[d])

    def gather_wait(q, buf, r):
        for d in (0, 1):
            got(buf.at[q, (y + 2) % 4, pl.ds(d * 64, 64)], r.at[q, 2 + d])

    def S1(q):
        got(F.at[q, y, pl.ds(0, 112)], pr.at[q])
        gather_first(q, F, ys, yr)

    def S2(q):
        gather_second(q, F, ys, yr)

    def S3(q):
        gather_wait(q, F, yr)
        g = jnp.zeros((128, 256), F32)
        u = jnp.zeros((128, 256), F32)
        for k in range(4):
            rows = F[q, k]
            g = g + dot(rows, Wg[k * WID : (k + 1) * WID, :])
            u = u + dot(rows, Wu[k * WID : (k + 1) * WID, :])
        Hd[q, y] = (g / (1.0 + jnp.exp(-g)) * u).astype(BF)

    def H(q):
        gather_first(q, Hd, hs, hr)

    def S4(q):
        gather_second(q, Hd, hs, hr)

    def S5(q):
        gather_wait(q, Hd, hr)
        o = jnp.zeros((128, WID), F32)
        for k in range(4):
            o = o + dot(Hd[q, k], Wd[k])
        O[q] = o.astype(BF)
        for j in range(1, 8):
            k, dev = in_plane(j)
            src = O.at[q, pl.ds(pl.multiple_of(k * 16, 16), 16)]
            dst = R.at[q, pl.ds(pl.multiple_of(m * 16, 16), 16)]
            pltpu.make_async_remote_copy(
                src_ref=src, dst_ref=dst, send_sem=qs.at[q], recv_sem=qr.at[q], device_id=dev, device_id_type=MESH
            ).start()
        mine = pl.ds(pl.multiple_of(m * 16, 16), 16)
        R[q, mine, :] = O[q, mine, :]
        sent.append(lambda: got(O.at[q, pl.ds(0, 112)], qs.at[q]))

    def S6(q):
        got(R.at[q, pl.ds(0, 112)], qr.at[q])
        if 1 <= q <= NEAR:
            target, side = pair_target()
            for d in (0, 1):
                CB[d, q - 1] = mix(weights(MT[d, q - 1], target, side == d), R[q])
            return
        k = lax.broadcasted_iota(jnp.int32, (128, 128), 0)
        r = lax.broadcasted_iota(jnp.int32, (128, 128), 1)
        slot, side = (r >> 4) * 8 + (r & 7), (r >> 3) & 1
        j = (q - 5) % 8
        DI[j] = dot(as_hot(k == side * 64 + slot), R[q]).astype(BF)
        for d in (0, 1):
            if q:
                rows, to = pl.ds(d * 64, 64), pl.ds(j * 64, 64)
            else:
                rows, to = pl.ds(64 + d * 32, 32), pl.ds(192, 32)
            send(DI.at[j, rows], FB.at[d, to], bs.at[d, j], br.at[d, j], along_z(1 - d, j + 1))

    def arrive(h, k):
        for d in (0, 1):
            got(piece(TR.at[d, h - 1], k), zr.at[d, h - 1, k])
            if h < NEAR:
                z_send(d, h, k)

    def far_out():
        for d in (0, 1):
            FS[d] = dot(as_hot(chosen(MT[d, NEAR - 1], far_target(d))), TR[d, NEAR - 1]).astype(BF)
        for j in range(4):
            for d in (0, 1):
                rows = pl.ds(j * 64, 64 if j < 3 else 32)
                to = pl.ds(d * 64, 64) if j < 3 else pl.ds(d * 32, 32)
                send(FS.at[d, rows], FR.at[j, to], fs.at[d, j], fr.at[d, j], along_z(d, j + 1))

    def meta_of(h):
        for d in (0, 1):
            got(MT.at[d, h - 1], mr.at[d, h - 1])

    PK[0] = select(MO[...], tok[...], 0).astype(BF)

    def forward_down():
        for d in (0, 1):
            got(ST.at[d], dr.at[d])
            send(ST.at[d], Wd.at[(y + (3, 1)[d]) % 4, pl.ds(d * 128, 128)], ds.at[4 + d], dr.at[4 + d], y_next[d])

    def down_there():
        for load in loads:
            load.wait()
        for d in (0, 1):
            got(Wd.at[(y + (3, 1)[d]) % 4], dr.at[2 + d])
            got(Wd.at[(y + 2) % 4, pl.ds(d * 128, 128)], dr.at[4 + d])

    arrive(1, 0), arrive(1, 1), meta_of(1), S0(1)
    forward_down()
    arrive(2, 0), S1(1), arrive(2, 1), meta_of(2), S0(2)
    arrive(3, 0), S1(2), S2(1), arrive(3, 1), meta_of(3), S0(3)
    arrive(4, 0), S1(3), S2(2), arrive(4, 1), meta_of(4), far_out(), S0(4)
    down_there()
    S2(3), S1(4), S0(5), S3(1), S3(2), S1(5), S0(6), S2(4), S3(3)
    S1(6), S0(7), S2(5), S3(4), S1(7), S0(0), S2(6), S3(5), H(5)
    S1(0), S2(7), S3(6), H(6), S4(5), S2(0), S3(7), H(7), S4(6), S5(5)
    S3(0), H(0), S4(7), S5(6), S6(5), H(4), S4(0), S5(7), S6(6)
    S4(4), H(3), H(2), H(1), S5(0), S6(7), S5(4), S6(0)
    S4(3), S6(4), S5(3), S4(2), S4(1)
    drain()
    def back(d, h, k, value):
        RO[d, h - 1, k * part : (k + 1) * part, :] = value.astype(BF)
        send(
            piece(RO.at[d, h - 1], k), piece(RA.at[d, h - 1], k), rs.at[d, h - 1, k], rr.at[d, h - 1, k], along_z(1 - d, 1)
        )

    for d in (0, 1):
        for j in range(4):
            to = pl.ds(j * 64, 64) if j < 3 else pl.ds(192, 32)
            got(FB.at[d, to], br.at[d, j])
        total = CB[d, NEAR - 1] + mix(weights(MT[d, NEAR - 1], far_target(d)), FB[d])
        for k in range(CUT):
            back(d, NEAR, k, total[k * part : (k + 1) * part])
    S6(3), S5(2), S5(1)

    def inwards(h):
        for k in range(CUT):
            for d in (0, 1):
                got(piece(RA.at[d, h], k), rr.at[d, h, k])
                rows = slice(k * part, (k + 1) * part)
                back(d, h, k, RA[d, h, rows, :].astype(F32) + CB[d, h - 1, rows, :])

    inwards(3)
    S6(2)
    inwards(2)
    S6(1)
    inwards(1)
    target, side = pair_target()
    CO[...] = mix(weights(MO[...], target, side == 0), R[0])
    drain()
    for k in range(CUT):
        for d in (0, 1):
            got(piece(RA.at[d, 0], k), rr.at[d, 0, k])
        rows = slice(k * part, (k + 1) * part)
        out[rows, :] = (
            CO[rows, :] + RA[0, 0, rows, :].astype(F32) + RA[1, 0, rows, :].astype(F32)
        ).astype(BF)


def body(tokens, expert_ids, route_weights, gate_weight, up_weight, down_weight):
    vmem = pl.BlockSpec(memory_space=pltpu.VMEM)
    hbm = pl.BlockSpec(memory_space=pl.ANY)
    V, DMA = pltpu.VMEM, pltpu.SemaphoreType.DMA
    scratch = [
        V((2, NEAR, TOK, WID), BF),
        V((8, TOK), F32),
        V((2, NEAR, 8, TOK), F32),
        V((PAIRS, 128, WID), BF),
        V((2, FAR_ROWS, WID), BF),
        V((4, 128, WID), BF),
        V((PAIRS, 4, 128, WID), BF),
        V((2048, 256), BF),
        V((2048, 256), BF),
        V((4, 256, WID), BF),
        V((2, 128, WID), BF),
        V((PAIRS, 4, 128, 256), BF),
        V((PAIRS, 128, WID), BF),
        V((PAIRS, 128, WID), BF),
        V((4, 128, WID), BF),
        V((2, FAR_ROWS, WID), BF),
        V((2, NEAR, TOK, WID), F32),
        V((TOK, WID), F32),
        V((2, NEAR, TOK, WID), BF),
        V((2, NEAR, TOK, WID), BF),
        DMA((3,)),
        DMA((2, NEAR, CUT)), DMA((2, NEAR, CUT)),
        DMA((2, NEAR)), DMA((2, NEAR)),
        DMA((2, 4)), DMA((2, 4)),
        DMA((PAIRS,)), DMA((PAIRS,)),
        DMA((PAIRS, 4)), DMA((PAIRS, 4)),
        DMA((PAIRS, 4)), DMA((PAIRS, 4)),
        DMA((6,)), DMA((6,)),
        DMA((PAIRS,)), DMA((PAIRS,)),
        DMA((2, 4)), DMA((2, 4)),
        DMA((2, NEAR, CUT)), DMA((2, NEAR, CUT)),
    ]
    return pl.pallas_call(
        kernel,
        out_shape=jax.ShapeDtypeStruct((TOK, WID), BF),
        in_specs=[vmem, vmem, vmem, hbm, hbm, hbm],
        out_specs=vmem,
        scratch_shapes=scratch,
        compiler_params=pltpu.CompilerParams(
            collective_id=0, has_side_effects=True, vmem_limit_bytes=60 * 1024 * 1024
        ),
        cost_estimate=pl.CostEstimate(
            flops=2 * 1024 * 3 * 2048 * 256, bytes_accessed=4 * 1024 * 1024, transcendentals=1024 * 256
        ),
    )(tokens, expert_ids.T, route_weights.T, gate_weight, up_weight, down_weight)


def solution(mesh):
    return jax.shard_map(
        body,
        mesh=mesh,
        in_specs=(
            P("dp", "tensor"),
            P("dp", None),
            P("dp", None),
            P("dp", None, "tensor"),
            P("dp", None, "tensor"),
            P("dp", "tensor", None),
        ),
        out_specs=P("dp", "tensor"),
        check_vma=False,
    )
```

```python
import jax
import jax.numpy as jnp
from jax import lax
from jax.experimental import pallas as pl
from jax.experimental.pallas import tpu as pltpu
from jax.sharding import PartitionSpec as P

MESH = pl.DeviceIdType.MESH
BF = jnp.bfloat16
F32 = jnp.float32
TOK = 256
WID = 512
CUT = 2
OUT = 4
BACK = 3
NEAR = max(OUT, BACK)
PAIRS = 8


def far_rows(near):
    return 64 * (7 - near) + 32


def far_index(q, near):
    return q - near - 1 if q else 7 - near


def far_slices(j, near, d):
    if j < 7 - near:
        return pl.ds(j * 64, 64), pl.ds(d * 64, 64)
    return pl.ds(j * 64, 32), pl.ds(d * 32, 32)


def dot(a, b):
    return jnp.dot(a, b, preferred_element_type=F32)


def dot_t(a, b):
    return lax.dot_general(a, b, (((0,), (0,)), ((), ())), preferred_element_type=F32)


def kernel(
    tok, ids, rw, gate_hbm, up_hbm, down_hbm, out,
    TR, MO, MT, PK, FS, FR, F, Wg, Wu, Wd, ST, Hd, O, R, DI, FB, CB, CO, RA, RO,
    wl, zs, zr, ms, mr, fs, fr, ps, pr, ys, yr, hs, hr, ds, dr, qs, qr, bs, br, rs, rr,
):
    dp = lax.axis_index("dp")
    y = lax.axis_index("tensor")
    x, z, c = dp // 32, (dp // 2) % 16, dp % 2
    m = x * 2 + c

    def at(x1, z1, c1):
        return ((x1 * 16 + z1) * 2 + c1, y)

    def along_z(d, h):
        return at(x, (z + (h if d == 0 else 16 - h)) % 16, c)

    def in_plane(j):
        k = (m + j) % 8
        return k, at(k // 2, z, k % 2)

    y_next = [(dp, (y + 1) % 4), (dp, (y + 3) % 4)]
    sent = []

    def send(src, dst, s, r, dev):
        copy = pltpu.make_async_remote_copy(
            src_ref=src, dst_ref=dst, send_sem=s, recv_sem=r, device_id=dev, device_id_type=MESH
        )
        copy.start()
        sent.append(copy.wait_send)

    def got(dst, r):
        pltpu.make_async_copy(dst, dst, r).wait()

    def drain():
        while sent:
            sent.pop()()

    loads = [
        pltpu.make_async_copy(gate_hbm.at[0], Wg, wl.at[0]),
        pltpu.make_async_copy(up_hbm.at[0], Wu, wl.at[1]),
        pltpu.make_async_copy(down_hbm.at[0, :, pl.ds(pl.multiple_of(y * WID, WID), WID)], Wd.at[y], wl.at[2]),
    ]
    for load in loads:
        load.start()

    barrier = pltpu.get_barrier_semaphore()
    peers = [along_z(d, h) for d in (0, 1) for h in range(1, 9 - min(OUT, BACK))]
    peers += [in_plane(j)[1] for j in range(1, 8)] + y_next
    for dev in peers:
        pl.semaphore_signal(barrier, inc=1, device_id=dev, device_id_type=MESH)
    pl.semaphore_wait(barrier, len(peers))

    part = TOK // CUT

    def piece(ref, k):
        return ref.at[pl.ds(k * part, part)]

    def z_send(d, h, k):
        src = tok if h == 0 else TR.at[d, h - 1]
        send(piece(src, k), piece(TR.at[d, h], k), zs.at[d, h, k], zr.at[d, h, k], along_z(d, 1))

    for k in range(CUT):
        for d in (0, 1):
            z_send(d, 0, k)

    def columns(j):
        return pl.ds(pl.multiple_of(((y + j) % 4) * WID, WID), WID)

    for d in (0, 1):
        send(down_hbm.at[0, pl.ds(d * 128, 128), columns(2)], ST.at[d], ds.at[d], dr.at[d], y_next[d])
    for d in (0, 1):
        send(down_hbm.at[0, :, columns((1, 3)[d])], Wd.at[y], ds.at[2 + d], dr.at[2 + d], y_next[d])

    row = lax.broadcasted_iota(jnp.int32, (128, TOK), 0)
    hot = [(row == ids[k : k + 1, :]).astype(F32) for k in (0, 1)]
    before = (
        lax.broadcasted_iota(jnp.int32, (TOK, TOK), 0) < lax.broadcasted_iota(jnp.int32, (TOK, TOK), 1)
    ).astype(F32).astype(BF)
    count = [dot(hot[k].astype(BF), before) for k in (0, 1)]
    count[1] = count[1] + jnp.sum(hot[0], axis=1, keepdims=True)
    MO[...] = jnp.zeros((8, TOK), F32)
    for k in (0, 1):
        e = ids[k : k + 1, :]
        rank = jnp.sum(hot[k] * count[k], axis=0, keepdims=True)
        place = ((e >> 1) & 15) * 64 + ((e >> 5) * 2 + (e & 1)) * 8
        MO[k : k + 1, :] = place.astype(F32) + rank
        MO[2 + k : 3 + k, :] = rw[k : k + 1, :]
    for h in range(NEAR):
        for d in (0, 1):
            send(MO, MT.at[d, h], ms.at[d, h], mr.at[d, h], along_z(d, h + 1))

    def pair_target():
        r = lax.broadcasted_iota(jnp.int32, (128, TOK), 0)
        return (z * 64 + (r >> 4) * 8 + (r & 7)).astype(F32), (r >> 3) & 1

    def far_target(d, near):
        r = lax.broadcasted_iota(jnp.int32, (far_rows(near), TOK), 0)
        step = (r >> 6) + 1
        station = (z + (step if d == 0 else 16 - step)) & 15
        within = r & 63
        if d == 1:
            within = jnp.where(r >= 64 * (7 - near), within + 32, within)
        return (station * 64 + within).astype(F32)

    def chosen(meta, target):
        return (meta[0:1, :] == target) | (meta[1:2, :] == target)

    def weights(meta, target, keep=None):
        w = jnp.where(meta[0:1, :] == target, meta[2:3, :], 0.0) + jnp.where(
            meta[1:2, :] == target, meta[3:4, :], 0.0
        )
        if keep is not None:
            w = jnp.where(keep, w, 0.0)
        high = w.astype(BF)
        return high, (w - high.astype(F32)).astype(BF)

    def mix(w, rows):
        return dot_t(w[0], rows) + dot_t(w[1], rows)

    def as_hot(mask):
        return jnp.where(mask, 1.0, 0.0).astype(BF)

    def select(meta, rows, d):
        target, side = pair_target()
        return dot(as_hot(chosen(meta, target) & (side == d)), rows)

    def to_plane(q):
        for j in range(1, 8):
            k, dev = in_plane(j)
            src = PK.at[q, pl.ds(pl.multiple_of(k * 16, 16), 16)]
            dst = F.at[q, y, pl.ds(pl.multiple_of(m * 16, 16), 16)]
            pltpu.make_async_remote_copy(
                src_ref=src, dst_ref=dst, send_sem=ps.at[q], recv_sem=pr.at[q], device_id=dev, device_id_type=MESH
            ).start()
        mine = pl.ds(pl.multiple_of(m * 16, 16), 16)
        F[q, y, mine, :] = PK[q, mine, :]
        sent.append(lambda: got(PK.at[q, pl.ds(0, 112)], ps.at[q]))

    def S0(q):
        if 1 <= q <= OUT:
            pick = select(MT[0, q - 1], TR[0, q - 1], 0) + select(MT[1, q - 1], TR[1, q - 1], 1)
        else:
            r = lax.broadcasted_iota(jnp.int32, (128, 128), 0)
            k = lax.broadcasted_iota(jnp.int32, (128, 128), 1)
            slot, side = (r >> 4) * 8 + (r & 7), (r >> 3) & 1
            j = far_index(q, OUT)
            if q:
                for d in (0, 1):
                    got(FR.at[j, pl.ds(d * 64, 64)], fr.at[d, j])
                pick = dot(as_hot(k == side * 64 + slot), FR[j])
            else:
                for d in (0, 1):
                    got(FR.at[j, pl.ds(d * 32, 32)], fr.at[d, j])
                pick = dot(as_hot((k == slot) & (side == 1)[:, :])[:, :64], FR[j, :64]) + PK[0].astype(F32)
        PK[q] = pick.astype(BF)
        to_plane(q)

    def gather_first(q, buf, s, r):
        for d in (0, 1):
            send(buf.at[q, y], buf.at[q, y], s.at[q, d], r.at[q, d], y_next[d])

    def gather_second(q, buf, s, r):
        for d in (0, 1):
            origin = (y + (3, 1)[d]) % 4
            got(buf.at[q, origin], r.at[q, d])
            half = buf.at[q, origin, pl.ds(d * 64, 64)]
            send(half, half, s.at[q, 2 + d], r.at[q, 2 + d], y_next[d])

    def gather_wait(q, buf, r):
        for d in (0, 1):
            got(buf.at[q, (y + 2) % 4, pl.ds(d * 64, 64)], r.at[q, 2 + d])

    def S1(q):
        got(F.at[q, y, pl.ds(0, 112)], pr.at[q])
        gather_first(q, F, ys, yr)

    def S2(q):
        gather_second(q, F, ys, yr)

    def S3(q):
        gather_wait(q, F, yr)
        g = jnp.zeros((128, 256), F32)
        u = jnp.zeros((128, 256), F32)
        for k in range(4):
            rows = F[q, k]
            g = g + dot(rows, Wg[k * WID : (k + 1) * WID, :])
            u = u + dot(rows, Wu[k * WID : (k + 1) * WID, :])
        Hd[q, y] = (g / (1.0 + jnp.exp(-g)) * u).astype(BF)

    def H(q):
        gather_first(q, Hd, hs, hr)

    def S4(q):
        gather_second(q, Hd, hs, hr)

    def S5(q):
        gather_wait(q, Hd, hr)
        o = jnp.zeros((128, WID), F32)
        for k in range(4):
            o = o + dot(Hd[q, k], Wd[k])
        O[q] = o.astype(BF)
        for j in range(1, 8):
            k, dev = in_plane(j)
            src = O.at[q, pl.ds(pl.multiple_of(k * 16, 16), 16)]
            dst = R.at[q, pl.ds(pl.multiple_of(m * 16, 16), 16)]
            pltpu.make_async_remote_copy(
                src_ref=src, dst_ref=dst, send_sem=qs.at[q], recv_sem=qr.at[q], device_id=dev, device_id_type=MESH
            ).start()
        mine = pl.ds(pl.multiple_of(m * 16, 16), 16)
        R[q, mine, :] = O[q, mine, :]
        sent.append(lambda: got(O.at[q, pl.ds(0, 112)], qs.at[q]))

    def S6(q):
        got(R.at[q, pl.ds(0, 112)], qr.at[q])
        if 1 <= q <= BACK:
            target, side = pair_target()
            for d in (0, 1):
                CB[d, q - 1] = mix(weights(MT[d, q - 1], target, side == d), R[q])
            return
        k = lax.broadcasted_iota(jnp.int32, (128, 128), 0)
        r = lax.broadcasted_iota(jnp.int32, (128, 128), 1)
        slot, side = (r >> 4) * 8 + (r & 7), (r >> 3) & 1
        j = far_index(q, BACK)
        DI[j] = dot(as_hot(k == side * 64 + slot), R[q]).astype(BF)
        for d in (0, 1):
            to, rows = far_slices(j, BACK, d)
            if not q:
                rows = pl.ds(64 + d * 32, 32)
            send(DI.at[j, rows], FB.at[d, to], bs.at[d, j], br.at[d, j], along_z(1 - d, j + 1))

    def arrive(h, k):
        for d in (0, 1):
            got(piece(TR.at[d, h - 1], k), zr.at[d, h - 1, k])
            if h < OUT:
                z_send(d, h, k)

    def far_out():
        for d in (0, 1):
            FS[d] = dot(as_hot(chosen(MT[d, OUT - 1], far_target(d, OUT))), TR[d, OUT - 1]).astype(BF)
        for j in range(8 - OUT):
            for d in (0, 1):
                rows, to = far_slices(j, OUT, d)
                send(FS.at[d, rows], FR.at[j, to], fs.at[d, j], fr.at[d, j], along_z(d, j + 1))

    def meta_of(h):
        for d in (0, 1):
            got(MT.at[d, h - 1], mr.at[d, h - 1])

    PK[0] = select(MO[...], tok[...], 0).astype(BF)

    def forward_down():
        for d in (0, 1):
            got(ST.at[d], dr.at[d])
            send(ST.at[d], Wd.at[(y + (3, 1)[d]) % 4, pl.ds(d * 128, 128)], ds.at[4 + d], dr.at[4 + d], y_next[d])

    def down_there():
        for load in loads:
            load.wait()
        for d in (0, 1):
            got(Wd.at[(y + (3, 1)[d]) % 4], dr.at[2 + d])
            got(Wd.at[(y + 2) % 4, pl.ds(d * 128, 128)], dr.at[4 + d])

    arrive(1, 0), arrive(1, 1), meta_of(1), S0(1)
    forward_down()
    arrive(2, 0), S1(1), arrive(2, 1), meta_of(2), S0(2)
    arrive(3, 0), S1(2), S2(1), arrive(3, 1), meta_of(3), S0(3)
    arrive(4, 0), S1(3), S2(2), arrive(4, 1), meta_of(4), far_out(), S0(4)
    down_there()
    S2(3), S1(4), S0(5), S3(1), S3(2), S1(5), S0(6), S2(4), S3(3)
    S1(6), S0(7), S2(5), S3(4), S1(7), S0(0), S2(6), S3(5), H(4), H(5)
    S1(0), S2(7), S3(6), H(6), S4(4), S4(5), S2(0), S3(7), H(7), S5(4), S4(6), S5(5)
    S3(0), H(0), S4(7), S6(4), S5(6), S6(5), H(3), S4(0), S5(7), S6(6)
    S4(3), H(2), H(1), S5(0), S6(7), S5(3), S6(0), S6(3)
    S4(2), S4(1)
    def back(d, h, k, value):
        RO[d, h - 1, k * part : (k + 1) * part, :] = value.astype(BF)
        send(
            piece(RO.at[d, h - 1], k), piece(RA.at[d, h - 1], k), rs.at[d, h - 1, k], rr.at[d, h - 1, k], along_z(1 - d, 1)
        )

    for d in (0, 1):
        for j in range(8 - BACK):
            got(FB.at[d, far_slices(j, BACK, d)[0]], br.at[d, j])
        total = CB[d, BACK - 1] + mix(weights(MT[d, BACK - 1], far_target(d, BACK)), FB[d])
        for k in range(CUT):
            back(d, BACK, k, total[k * part : (k + 1) * part])

    def inwards(h):
        for k in range(CUT):
            for d in (0, 1):
                got(piece(RA.at[d, h], k), rr.at[d, h, k])
                rows = slice(k * part, (k + 1) * part)
                back(d, h, k, RA[d, h, rows, :].astype(F32) + CB[d, h - 1, rows, :])

    S5(2), S5(1), S6(2)
    inwards(2)
    S6(1)
    inwards(1)
    target, side = pair_target()
    CO[...] = mix(weights(MO[...], target, side == 0), R[0])
    drain()
    for k in range(CUT):
        for d in (0, 1):
            got(piece(RA.at[d, 0], k), rr.at[d, 0, k])
        rows = slice(k * part, (k + 1) * part)
        out[rows, :] = (
            CO[rows, :] + RA[0, 0, rows, :].astype(F32) + RA[1, 0, rows, :].astype(F32)
        ).astype(BF)


def body(tokens, expert_ids, route_weights, gate_weight, up_weight, down_weight):
    vmem = pl.BlockSpec(memory_space=pltpu.VMEM)
    hbm = pl.BlockSpec(memory_space=pl.ANY)
    V, DMA = pltpu.VMEM, pltpu.SemaphoreType.DMA
    scratch = [
        V((2, OUT, TOK, WID), BF),
        V((8, TOK), F32),
        V((2, NEAR, 8, TOK), F32),
        V((PAIRS, 128, WID), BF),
        V((2, far_rows(OUT), WID), BF),
        V((8 - OUT, 128, WID), BF),
        V((PAIRS, 4, 128, WID), BF),
        V((2048, 256), BF),
        V((2048, 256), BF),
        V((4, 256, WID), BF),
        V((2, 128, WID), BF),
        V((PAIRS, 4, 128, 256), BF),
        V((PAIRS, 128, WID), BF),
        V((PAIRS, 128, WID), BF),
        V((8 - BACK, 128, WID), BF),
        V((2, far_rows(BACK), WID), BF),
        V((2, BACK, TOK, WID), F32),
        V((TOK, WID), F32),
        V((2, BACK, TOK, WID), BF),
        V((2, BACK, TOK, WID), BF),
        DMA((3,)),
        DMA((2, OUT, CUT)), DMA((2, OUT, CUT)),
        DMA((2, NEAR)), DMA((2, NEAR)),
        DMA((2, 8 - OUT)), DMA((2, 8 - OUT)),
        DMA((PAIRS,)), DMA((PAIRS,)),
        DMA((PAIRS, 4)), DMA((PAIRS, 4)),
        DMA((PAIRS, 4)), DMA((PAIRS, 4)),
        DMA((6,)), DMA((6,)),
        DMA((PAIRS,)), DMA((PAIRS,)),
        DMA((2, 8 - BACK)), DMA((2, 8 - BACK)),
        DMA((2, BACK, CUT)), DMA((2, BACK, CUT)),
    ]
    return pl.pallas_call(
        kernel,
        out_shape=jax.ShapeDtypeStruct((TOK, WID), BF),
        in_specs=[vmem, vmem, vmem, hbm, hbm, hbm],
        out_specs=vmem,
        scratch_shapes=scratch,
        compiler_params=pltpu.CompilerParams(
            collective_id=0, has_side_effects=True, vmem_limit_bytes=60 * 1024 * 1024
        ),
        cost_estimate=pl.CostEstimate(
            flops=2 * 1024 * 3 * 2048 * 256, bytes_accessed=4 * 1024 * 1024, transcendentals=1024 * 256
        ),
    )(tokens, expert_ids.T, route_weights.T, gate_weight, up_weight, down_weight)


def solution(mesh):
    return jax.shard_map(
        body,
        mesh=mesh,
        in_specs=(
            P("dp", "tensor"),
            P("dp", None),
            P("dp", None),
            P("dp", None, "tensor"),
            P("dp", None, "tensor"),
            P("dp", "tensor", None),
        ),
        out_specs=P("dp", "tensor"),
        check_vma=False,
    )
```
